128 devices in a mesh: seq: 8 (over x, core), res: 16 (over z, y).
Axes of the slice: x: 4, y: 4, z: 4, core: 2. Of those that a mesh axis runs over, the one named last changes fastest.
Arguments:
- normed: bfloat16 [512, 256, 768], P('seq', 'res'), may hold values from -8 to 8
- cotangent: bfloat16 [512, 256, 768], P('seq', 'res'), may hold values from -40 to 40
- w_query: bfloat16 [768, 768], replicated, may hold values from -0.16237976 to 0.16237976
- w_key: bfloat16 [768, 768], replicated, may hold values from -0.16237976 to 0.16237976
- w_value: bfloat16 [768, 768], replicated, may hold values from -0.21875 to 0.21875
- w_out: bfloat16 [768, 768], replicated, may hold values from -0.21875 to 0.21875
Outputs:
- input_grad: bfloat16 [512, 256, 768], P('seq', 'res')
The draws below stay inside these ranges and needn't reach their ends.
All inputs are finite; a program needn't handle non-finite values.
Results may differ from the reference program's by a relative error of at most 0.0085.
Values may be sent and summed in bfloat16 or wider, within the bound.
No kernel may reach another device: no remote copies, remote signals or barrier semaphores. Data moves between devices by JAX's collectives and lax.ppermute only.
A program may use at most 64 MiB of HBM per device.

```python
import math
import jax
import jax.numpy as jnp
from jax import lax

D = 768
HEADS = 12
HEAD = 64
SEQS = 512
RES = 256


def draw_normed(key, part):
    key = jax.random.fold_in(key, 11)
    full_shape = (SEQS, RES, D)
    drawn = jnp.clip(jax.random.normal(key, full_shape, jnp.float32), -4.0, 4.0)
    return drawn.astype(jnp.bfloat16)


def draw_w_query(key, part):
    key = jax.random.fold_in(key, 23)
    private = jnp.clip(jax.random.normal(key, (D, D), jnp.float32), -4.0, 4.0) / math.sqrt(D)
    matrix = private
    return matrix.astype(jnp.bfloat16)


def draw_w_key(key, part):
    key = jax.random.fold_in(key, 37)
    private = jnp.clip(jax.random.normal(key, (D, D), jnp.float32), -4.0, 4.0) / math.sqrt(D)
    matrix = private
    return matrix.astype(jnp.bfloat16)


def block_scale(rng, dims, pieces, least, largest):
    level, own = 1.0, jax.random.fold_in(rng, 6)
    for dim, shards_of in pieces:
        steps = jnp.exp(jax.random.uniform(jax.random.fold_in(own, dim), (shards_of,), jnp.float32, least / len(pieces), largest / len(pieces)))
        level = level * jnp.repeat(steps, dims[dim] // shards_of).reshape([-1 if axis == dim else 1 for axis in range(len(dims))])
    return level


def normal_values(stream_key, dims, scale, limit, cuts=(), held_as=jnp.bfloat16):
    entries = scale * jax.random.normal(stream_key, dims, jnp.float32)
    if cuts:
        entries = entries * block_scale(stream_key, dims, cuts, -0.22, 0.18)
    return jnp.clip(entries, -limit, limit).astype(held_as)


def setup_inputs(seed: int = 0) -> dict:
    seeds = jax.random.split(jax.random.key(seed), 7)
    return {
        "normed": draw_normed(jax.random.fold_in(seeds[6], 71), 0),
        "cotangent": normal_values(seeds[1], (SEQS, RES, D), 8.0, 40.0, ((0, 8), (1, 16))),
        "w_query": draw_w_query(jax.random.fold_in(seeds[6], 71), 0),
        "w_key": draw_w_key(jax.random.fold_in(seeds[6], 71), 0),
        "w_value": normal_values(seeds[4], (D, D), D ** -0.5, 0.21875),
        "w_out": normal_values(seeds[5], (D, D), D ** -0.5, 0.21875),
    }


def widen(array):
    return array.astype(jnp.float32)

def softmax_backward(tied_logit, prob_grad, scaling):
    row_max = lax.optimization_barrier(jnp.max(tied_logit, axis=-1, keepdims=True))
    exponent = jnp.exp(tied_logit - row_max)
    attn_prob = (exponent / lax.optimization_barrier(jnp.sum(exponent, axis=-1, keepdims=True))).astype(jnp.bfloat16)
    weights = attn_prob.astype(jnp.float32)
    row_dot = lax.optimization_barrier(jnp.sum(weights * prob_grad, axis=-1, keepdims=True))
    logit_grad = (scaling * weights * (prob_grad - row_dot)).astype(jnp.bfloat16)
    return (attn_prob, logit_grad)

def reference(normed, cotangent, w_query, w_key, w_value, w_out):
    scaling = 1.0 / math.sqrt(HEAD * SEQS)
    flat_input = normed.reshape(SEQS * RES, D)

    def project(matrix):
        product = jnp.dot(flat_input, matrix, preferred_element_type=jnp.float32)
        return product.astype(jnp.bfloat16).reshape(SEQS, RES, HEADS, HEAD)
    query_rows = project(w_query)
    key_rows = project(w_key)
    value_rows = project(w_value)
    out_grad = jnp.dot(cotangent.reshape(SEQS * RES, D), w_out.T, preferred_element_type=jnp.float32)
    out_grad = out_grad.astype(jnp.bfloat16).reshape(SEQS, RES, HEADS, HEAD)
    tied_logit = scaling * jnp.einsum('sihe,sjhe->ihj', widen(query_rows), widen(key_rows))
    prob_grad = jnp.einsum('sihe,sjhe->ihj', widen(out_grad), widen(value_rows))
    attn_prob, logit_grad = softmax_backward(tied_logit, prob_grad, scaling)
    query_grad = jnp.einsum('ihj,sjhe->sihe', widen(logit_grad), widen(key_rows)).astype(jnp.bfloat16)
    key_grad = jnp.einsum('ihj,sihe->sjhe', widen(logit_grad), widen(query_rows)).astype(jnp.bfloat16)
    value_grad = jnp.einsum('ihj,sihe->sjhe', widen(attn_prob), widen(out_grad)).astype(jnp.bfloat16)
    total = jnp.dot(query_grad.reshape(SEQS * RES, D), w_query.T, preferred_element_type=jnp.float32)
    total = total + jnp.dot(key_grad.reshape(SEQS * RES, D), w_key.T, preferred_element_type=jnp.float32)
    total = total + jnp.dot(value_grad.reshape(SEQS * RES, D), w_value.T, preferred_element_type=jnp.float32)
    return total.astype(jnp.bfloat16).reshape(SEQS, RES, D)
```

```python
import math

import jax
import jax.numpy as jnp
from jax import lax
from jax.experimental import pallas as pl
from jax.experimental.pallas import tpu as pltpu
from jax.sharding import Mesh, PartitionSpec as P

HEADS = 12
F32 = jnp.float32
BF16 = jnp.bfloat16
VMEM = pl.BlockSpec(memory_space=pltpu.VMEM)
SMEM = pl.BlockSpec(memory_space=pltpu.SMEM)
PARAMS = pltpu.CompilerParams(vmem_limit_bytes=40 * 1024 * 1024)
NT = (((1,), (1,)), ((), ()))
TN = (((0,), (0,)), ((), ()))


def dot(a, b, dims=(((1,), (0,)), ((), ()))):
    return lax.dot_general(a, b, dims, preferred_element_type=F32)


def rows_of(x_ref, s):
    blocks, _, block, width = x_ref.shape
    return x_ref[:, s].reshape(blocks * block, width)


def project(x_ref, pairs):
    seqs = x_ref.shape[1]
    for s in range(seqs):
        rows = rows_of(x_ref, s)
        for w_ref, o_ref in pairs:
            heads, packed, res = o_ref.shape
            head = packed // seqs
            out = dot(w_ref[...], rows, NT).astype(BF16)
            o_ref[:, s * head : (s + 1) * head, :] = out.reshape(heads, head, res)


def pair_products(core, scale, a_ref, b_ref, own_ref, other_ref):
    half = own_ref.shape[0]
    for h in range(half):
        for ref, base in ((own_ref, core * half), (other_ref, (1 - core) * half)):
            product = dot(a_ref[base + h], b_ref[base + h], TN)
            ref[h] = product if scale is None else scale * product


def rows_kernel(scale, core_ref, x_ref, wq_ref, wk_ref, wv_ref, q_ref, k_ref, v_ref, own_ref, other_ref):
    project(x_ref, ((wq_ref, q_ref), (wk_ref, k_ref), (wv_ref, v_ref)))
    pair_products(core_ref[0], scale, q_ref, k_ref, own_ref, other_ref)


def grad_rows_kernel(core_ref, c_ref, w_ref, v_ref, g_ref, own_ref, other_ref):
    project(c_ref, ((w_ref, g_ref),))
    pair_products(core_ref[0], None, g_ref, v_ref, own_ref, other_ref)


def pack_kernel(*refs):
    out_ref = refs[-1]
    blocks, terms, heads, rows, res = out_ref.shape
    for t in range(terms):
        a_ref, b_ref = refs[2 * t : 2 * t + 2]
        for h in range(heads):
            out_ref[:, t, h] = (a_ref[h] + b_ref[h]).astype(out_ref.dtype).reshape(blocks, rows, res)


def fold_kernel(x_ref, out_ref):
    total = x_ref[0].astype(F32)
    for k in range(1, x_ref.shape[0]):
        total = total + x_ref[k].astype(F32)
    out_ref[...] = total


def softmax_kernel(scaling, a_ref, b_ref, c_ref, d_ref, out_ref):
    total = (a_ref[...] + b_ref[...]) + (c_ref[...] + d_ref[...])
    logit, grad = total[0], total[1]
    exponent = jnp.exp(logit - jnp.max(logit, axis=-1, keepdims=True))
    prob = (exponent / jnp.sum(exponent, axis=-1, keepdims=True)).astype(BF16)
    weights = prob.astype(F32)
    row_dot = jnp.sum(weights * grad, axis=-1, keepdims=True)
    logit_grad = (scaling * weights * (grad - row_dot)).astype(BF16)
    for k in range(out_ref.shape[0]):
        out_ref[k, 0] = prob
        out_ref[k, 1] = logit_grad


def output_kernel(core_ref, own_ref, other_ref, q_ref, k_ref, g_ref, wq_ref, wk_ref, wv_ref, out_ref, qg_ref, kg_ref, vg_ref):
    core = core_ref[0]
    half = own_ref.shape[2]
    res = own_ref.shape[-1]
    seqs = out_ref.shape[1]
    for h in range(half):
        for ref, base in ((own_ref, core * half), (other_ref, (1 - core) * half)):
            prob = ref[:, 0, h].reshape(res, res)
            logit_grad = ref[:, 1, h].reshape(res, res)
            hh = base + h
            for o_ref, value in (
                (qg_ref, dot(k_ref[hh], logit_grad, NT)),
                (kg_ref, dot(q_ref[hh], logit_grad)),
                (vg_ref, dot(g_ref[hh], prob)),
            ):
                o_ref[:, hh] = value.astype(BF16).reshape(seqs, -1, res)
    for s in range(seqs):
        total = None
        for w_ref, o_ref in ((wq_ref, qg_ref), (wk_ref, kg_ref), (wv_ref, vg_ref)):
            part = dot(w_ref[...], o_ref[s].reshape(-1, res))
            total = part if total is None else total + part
        out_ref[:, s] = total.astype(BF16).T.reshape(out_ref.shape[0], -1, out_ref.shape[-1])


def call(kernel, outs, *args, smem=0, scratch=()):
    return pl.pallas_call(
        kernel,
        out_shape=outs,
        in_specs=[SMEM] * smem + [VMEM] * (len(args) - smem),
        out_specs=jax.tree.map(lambda _: VMEM, outs),
        scratch_shapes=scratch,
        compiler_params=PARAMS,
    )(*args)


def shape(dims, dtype=BF16):
    return jax.ShapeDtypeStruct(dims, dtype)


def ring(axis, step):
    n = lax.axis_size(axis)
    return [(i, (i + step) % n) for i in range(n)]


def body(normed, cotangent, w_query, w_key, w_value, w_out):
    blocks = lax.axis_size(("z", "y"))
    seq_count, block, width = normed.shape
    seqs, res = seq_count // blocks, block * blocks
    head = width // HEADS
    half = HEADS // 2
    scaling = 1.0 / math.sqrt(head * seqs * lax.axis_size(("x", "core", "z", "y")))
    core = lax.axis_index("core").reshape(1).astype(jnp.int32)

    def exchange(a, axes=("z", "y")):
        return lax.all_to_all(a, axes, split_axis=0, concat_axis=0, tiled=True)

    rows = exchange(normed.reshape(blocks, seqs, block, width))
    cot_rows = exchange(cotangent.reshape(blocks, seqs, block, width))
    packed = shape((HEADS, seqs * head, res))
    sums = shape((half, res, res), F32)

    def swap(a):
        return lax.ppermute(a, "core", ring("core", 1))

    q, k, v, logit_own, logit_other = call(
        lambda *refs: rows_kernel(scaling, *refs),
        (packed, packed, packed, sums, sums),
        core, rows, w_query.T, w_key.T, w_value.T, smem=1,
    )
    logit_recv = swap(logit_other)
    g, grad_own, grad_other = call(
        grad_rows_kernel, (packed, sums, sums), core, cot_rows, w_out, v, smem=1
    )
    grad_recv = swap(grad_other)
    split = lax.axis_size(("x", "z"))
    cut = (2, half, res // split, res)
    terms = call(pack_kernel, shape((split,) + cut), logit_own, logit_recv, grad_own, grad_recv)
    terms = exchange(terms, ("x", "z"))
    term = call(fold_kernel, shape(cut, F32), terms)
    others = [lax.ppermute(term, "y", ring("y", step)) for step in (1, 2, 3)]
    result = call(lambda *refs: softmax_kernel(scaling, *refs), shape((split,) + cut), term, *others)
    result = exchange(result, ("x", "z"))
    result_other = swap(result)
    grads = pltpu.VMEM((seqs, HEADS, head, res), BF16)
    out = call(
        output_kernel,
        shape((blocks, seqs, block, width)),
        core, result, result_other, q, k, g, w_query, w_key, w_value,
        smem=1, scratch=[grads, grads, grads],
    )
    return exchange(out).reshape(seq_count, block, width)


def solution(mesh):
    fine = Mesh(mesh.devices.reshape(4, 2, 4, 4), ("x", "core", "z", "y"))
    spec = P(("x", "core"), ("z", "y"), None)
    return jax.shard_map(
        body, mesh=fine, in_specs=(spec, spec, P(), P(), P(), P()), out_specs=spec, check_vma=False
    )
```

```python
import math

import jax
import jax.numpy as jnp
from jax import lax
from jax.experimental import pallas as pl
from jax.experimental.pallas import tpu as pltpu
from jax.sharding import Mesh, PartitionSpec as P

HEADS = 12
F32 = jnp.float32
BF16 = jnp.bfloat16
VMEM = pl.BlockSpec(memory_space=pltpu.VMEM)
SMEM = pl.BlockSpec(memory_space=pltpu.SMEM)
HBM = pl.BlockSpec(memory_space=pltpu.HBM)
NT = (((1,), (1,)), ((), ()))
TN = (((0,), (0,)), ((), ()))


def dot(a, b, dims=(((1,), (0,)), ((), ()))):
    return lax.dot_general(a, b, dims, preferred_element_type=F32)


def project(x_ref, pairs):
    blocks, seqs, block, width = x_ref.shape
    for s in range(seqs):
        rows = x_ref[:, s].reshape(blocks * block, width)
        for w_ref, o_ref in pairs:
            heads, packed, res = o_ref.shape
            head = packed // seqs
            out = dot(w_ref[...], rows, NT).astype(BF16)
            o_ref[:, s * head : (s + 1) * head, :] = out.reshape(heads, head, res)


def pair_products(core, scale, a_ref, b_ref, own_ref, other_ref):
    half = own_ref.shape[0]
    for h in range(half):
        for ref, base in ((own_ref, core * half), (other_ref, (1 - core) * half)):
            product = dot(a_ref[base + h], b_ref[base + h], TN)
            ref[h] = product if scale is None else scale * product


def start(pairs, sems):
    copies = [pltpu.make_async_copy(src, dst, sems.at[n]) for n, (src, dst) in enumerate(pairs)]
    for copy in copies:
        copy.start()
    return copies


def rows_kernel(scale, place_ref, x_ref, wq_in, wk_in, q_out, k_out, own_ref, other_ref, wq, wk, t_ref, q_ref, k_ref, in_sems, out_sems):
    loads = start(((wq_in, wq), (wk_in, wk)), in_sems)
    for load, w, o_ref in zip(loads, (wq, wk), (q_ref, k_ref)):
        load.wait()
        t_ref[...] = w[...].T
        project(x_ref, ((t_ref, o_ref),))
    stores = start(((q_ref, q_out), (k_ref, k_out)), out_sems)
    pair_products(place_ref[0], scale, q_ref, k_ref, own_ref, other_ref)
    for store in stores:
        store.wait()


def value_kernel(x_ref, w_ref, v_ref, t_ref):
    t_ref[...] = w_ref[...].T
    project(x_ref, ((t_ref, v_ref),))


def grad_rows_kernel(place_ref, c_ref, w_in, v_in, g_out, own_ref, other_ref, w, v_ref, g_ref, in_sems, out_sems):
    loads = start(((w_in, w), (v_in, v_ref)), in_sems)
    loads[0].wait()
    project(c_ref, ((w, g_ref),))
    stores = start(((g_ref, g_out),), out_sems)
    loads[1].wait()
    pair_products(place_ref[0], None, g_ref, v_ref, own_ref, other_ref)
    stores[0].wait()


def split_kernel(place_ref, a_ref, b_ref, *outs):
    rows = outs[0].shape[0]
    for d, ref in enumerate(outs):
        at = pl.ds(pl.multiple_of(lax.rem(place_ref[1] + d, len(outs)) * rows, rows), rows)
        ref[...] = (a_ref[at] + b_ref[at]).astype(ref.dtype)


def sum_kernel(*refs):
    a, b, c, d, out_ref = refs
    out_ref[...] = (a[...] + b[...]) + (c[...] + d[...])


def fold_kernel(place_ref, logit_ref, *refs):
    grads, outs = refs[:4], refs[4:]
    rows = outs[0].shape[0] // 2
    for d, ref in enumerate(outs):
        at = pl.ds(pl.multiple_of(lax.rem(place_ref[2] + d, len(outs)) * rows, rows), rows)
        a, b, c, e = (grad[at].astype(F32) for grad in grads)
        ref[pl.ds(0, rows)] = logit_ref[at]
        ref[pl.ds(rows, rows)] = (a + b) + (c + e)


def softmax_kernel(scaling, a_ref, b_ref, c_ref, d_ref, out_ref):
    total = (a_ref[...] + b_ref[...]) + (c_ref[...] + d_ref[...])
    rows = total.shape[0] // 2
    logit, grad = total[:rows], total[rows:]
    exponent = jnp.exp(logit - jnp.max(logit, axis=-1, keepdims=True))
    prob = (exponent / jnp.sum(exponent, axis=-1, keepdims=True)).astype(BF16)
    weights = prob.astype(F32)
    row_dot = jnp.sum(weights * grad, axis=-1, keepdims=True)
    out_ref[pl.ds(0, rows)] = prob
    out_ref[pl.ds(rows, rows)] = (scaling * weights * (grad - row_dot)).astype(BF16)


def join_kernel(place_ref, *refs):
    parts, out_ref = refs[:-1], refs[-1]
    rows = out_ref.shape[1] // len(parts)
    for d, part_ref in enumerate(parts):
        first = lax.rem(place_ref[2] + len(parts) - d, len(parts)) * rows
        at = pl.ds(pl.multiple_of(first, rows), rows)
        for term in range(2):
            out_ref[term, at] = part_ref[pl.ds(term * rows, rows)]


def head_grads(base, here, parts, q_ref, k_ref, g_ref, outs, stage_ref):
    rows = parts[0].shape[1]
    for d, part_ref in enumerate(parts):
        first = lax.rem(here + len(parts) - d, len(parts)) * rows
        stage_ref[:, pl.ds(pl.multiple_of(first, rows), rows)] = part_ref[...].astype(F32)
    res = stage_ref.shape[-1]
    for h in range(q_ref.shape[0] // 2):
        prob, logit_grad = (stage_ref[term, pl.ds(h * res, res)].astype(BF16) for term in range(2))
        hh = base + h
        for o_ref, value in zip(
            outs,
            (dot(k_ref[hh], logit_grad, NT), dot(q_ref[hh], logit_grad), dot(g_ref[hh], prob)),
        ):
            o_ref[:, hh] = value.astype(BF16).reshape(o_ref.shape[0], -1, res)


def output_kernel(place_ref, *refs):
    own, other, held_in, weights_in, out_ref = refs[:4], refs[4:8], refs[8:11], refs[11:14], refs[14]
    held, weights, outs, stage_ref, sems = refs[15:18], refs[18:21], refs[21:24], refs[24], refs[25]
    loads = start(list(zip((*held_in, *weights_in), (*held, *weights))), sems)
    for load in loads[:3]:
        load.wait()
    core = place_ref[0]
    half = held[0].shape[0] // 2
    head_grads(core * half, place_ref[1], own, *held, outs, stage_ref)
    head_grads((1 - core) * half, place_ref[3], other, *held, outs, stage_ref)
    for load in loads[3:]:
        load.wait()
    res = held[0].shape[-1]
    for s in range(out_ref.shape[1]):
        total = None
        for w_ref, o_ref in zip(weights, outs):
            part = dot(w_ref[...], o_ref[s].reshape(-1, res))
            total = part if total is None else total + part
        out_ref[:, s] = total.astype(BF16).T.reshape(out_ref.shape[0], -1, out_ref.shape[-1])


def call(kernel, outs, *args, specs=None, out_specs=None, scratch=(), mib=16):
    return pl.pallas_call(
        kernel,
        out_shape=outs,
        in_specs=list(specs or [VMEM] * len(args)),
        out_specs=out_specs or jax.tree.map(lambda _: VMEM, outs),
        scratch_shapes=scratch,
        compiler_params=pltpu.CompilerParams(vmem_limit_bytes=mib * 1024 * 1024),
    )(*args)


def shape(dims, dtype=BF16):
    return jax.ShapeDtypeStruct(dims, dtype)


def shift(a, axis, step):
    n = lax.axis_size(axis)
    return lax.ppermute(a, axis, [(i, (i + step) % n) for i in range(n)])


AXES = ("x", "core", "z", "y")


def number(x, core, z, y):
    return x * 32 + core * 16 + z * 4 + y


def turn(stage, step):
    pairs = []
    for core, axes in ((0, "xzy"), (1, "yxz")):
        for n in range(64):
            at = dict(x=n // 16, z=n // 4 % 4, y=n % 4)
            to = dict(at)
            to[axes[stage]] = (at[axes[stage]] + step) % 4
            pairs.append((number(core=core, **at), number(core=core, **to)))
    return pairs


def body(normed, cotangent, w_query, w_key, w_value, w_out):
    blocks = lax.axis_size(("z", "y"))
    seq_count, block, width = normed.shape
    seqs, res = seq_count // blocks, block * blocks
    head = width // HEADS
    half = HEADS // 2
    scaling = 1.0 / math.sqrt(head * seqs * lax.axis_size(AXES))
    core, x, z, y = (lax.axis_index(axis) for axis in ("core", "x", "z", "y"))
    place = jnp.stack(
        [core, jnp.where(core == 0, x, y), jnp.where(core == 0, z, x), jnp.where(core == 0, y, x)]
    ).astype(jnp.int32)

    def exchange(a):
        return lax.all_to_all(a, ("z", "y"), split_axis=0, concat_axis=0, tiled=True)

    def spread(parts, stage):
        sent = {d: lax.ppermute(parts[d], AXES, turn(stage, d)) for d in (1, 3, 2)}
        return [parts[0]] + [sent[d] for d in (1, 2, 3)]

    def flat(a):
        return a.reshape(half * res, res)

    rows = exchange(normed.reshape(blocks, seqs, block, width))
    cot_rows = exchange(cotangent.reshape(blocks, seqs, block, width))
    packed = shape((HEADS, seqs * head, res))
    sums = shape((half, res, res), F32)
    quarter = (half * res // 4, res)
    weight, held = pltpu.VMEM((width, width), BF16), pltpu.VMEM(packed.shape, BF16)
    sems = pltpu.SemaphoreType.DMA

    def split(dtype, own, other):
        return call(
            split_kernel, [shape(quarter, dtype)] * 4, place, flat(own), flat(shift(other, "core", 1)),
            specs=(SMEM, VMEM, VMEM),
        )

    def row_part(rows, *weights):
        q, k, own, other = call(
            lambda *refs: rows_kernel(scaling, *refs),
            (packed, packed, sums, sums),
            place, rows, *weights[:2],
            specs=(SMEM, VMEM, HBM, HBM), out_specs=(HBM, HBM, VMEM, VMEM),
            scratch=[weight] * 3 + [held] * 2 + [sems((2,)), sems((2,))], mib=24,
        )
        v = call(value_kernel, packed, rows, weights[2], scratch=[weight])
        return q, k, v, call(sum_kernel, shape(quarter, F32), *spread(split(F32, own, other), 0))

    def no_part(*_):
        return *(jnp.zeros(packed.shape, BF16) for _ in range(3)), jnp.zeros(quarter, F32)

    q, k, v, logit = lax.cond(core < 2, row_part, no_part, rows, w_query, w_key, w_value)
    g, grad_own, grad_other = call(
        grad_rows_kernel, (packed, sums, sums), place, cot_rows, w_out, v,
        specs=(SMEM, VMEM, HBM, HBM), out_specs=(HBM, VMEM, VMEM),
        scratch=[weight, held, held, sems((2,)), sems((1,))],
    )
    grads = spread(split(BF16, grad_own, grad_other), 0)
    both = (quarter[0] // 2, res)
    terms = call(
        fold_kernel, [shape(both, F32)] * 4, place, logit, *grads, specs=[SMEM] + [VMEM] * 5
    )
    term = call(sum_kernel, shape(both, F32), *spread(terms, 1))
    result = call(
        lambda *refs: softmax_kernel(scaling, *refs), shape(both), *spread([term] * 4, 2)
    )
    result = call(
        join_kernel, shape((2,) + quarter), place, *spread([result] * 4, 1), specs=[SMEM] + [VMEM] * 4
    )
    own = spread([result] * 4, 0)
    other = [shift(a, "core", 1) for a in own]
    grown = pltpu.VMEM((seqs, HEADS, head, res), BF16)
    out = call(
        output_kernel,
        shape((blocks, seqs, block, width)),
        place, *own, *other, q, k, g, w_query, w_key, w_value,
        specs=[SMEM] + [VMEM] * 8 + [HBM] * 6,
        scratch=[held] * 3 + [weight] * 3 + [grown] * 3
        + [pltpu.VMEM((2, half * res, res), F32), sems((6,))],
        mib=40,
    )
    return exchange(out).reshape(seq_count, block, width)


def solution(mesh):
    fine = Mesh(mesh.devices.reshape(4, 2, 4, 4), ("x", "core", "z", "y"))
    spec = P(("x", "core"), ("z", "y"), None)
    return jax.shard_map(
        body, mesh=fine, in_specs=(spec, spec, P(), P(), P(), P()), out_specs=spec, check_vma=False
    )
```

```python
import math

import jax
import jax.numpy as jnp
from jax import lax
from jax.experimental import pallas as pl
from jax.experimental.pallas import tpu as pltpu
from jax.sharding import Mesh, PartitionSpec as P

HEADS = 12
F32 = jnp.float32
BF16 = jnp.bfloat16
VMEM = pl.BlockSpec(memory_space=pltpu.VMEM)
SMEM = pl.BlockSpec(memory_space=pltpu.SMEM)
ANY = pl.BlockSpec(memory_space=pl.ANY)
HBM = pl.BlockSpec(memory_space=pltpu.HBM)
NT = (((1,), (1,)), ((), ()))
TN = (((0,), (0,)), ((), ()))


def dot(a, b, dims=(((1,), (0,)), ((), ()))):
    return lax.dot_general(a, b, dims, preferred_element_type=F32)


def project(x_ref, pairs):
    blocks, seqs, block, width = x_ref.shape
    for s in range(seqs):
        rows = x_ref[:, s].reshape(blocks * block, width)
        for w_ref, o_ref in pairs:
            heads, packed, res = o_ref.shape
            head = packed // seqs
            out = dot(w_ref[...], rows, NT).astype(BF16)
            o_ref[:, s * head : (s + 1) * head, :] = out.reshape(heads, head, res)


def pair_products(core, scale, a_ref, b_ref, own_ref, other_ref):
    half = own_ref.shape[0]
    for h in range(half):
        for ref, base in ((own_ref, core * half), (other_ref, (1 - core) * half)):
            product = dot(a_ref[base + h], b_ref[base + h], TN)
            ref[h] = (product if scale is None else scale * product).astype(ref.dtype)


def start(pairs, sems):
    copies = [pltpu.make_async_copy(src, dst, sems.at[n]) for n, (src, dst) in enumerate(pairs)]
    for copy in copies:
        copy.start()
    return copies


def rows_kernel(scale, place_ref, x_in, wq_in, wk_in, q_out, k_out, own_ref, other_ref, wq, wk, t_ref, x_ref, q_ref, k_ref, in_sems, out_sems):
    loads = start(((wq_in, wq), (x_in, x_ref), (wk_in, wk)), in_sems)
    loads[0].wait()
    t_ref[...] = wq[...].T
    loads[1].wait()
    project(x_ref, ((t_ref, q_ref),))
    stores = start(((q_ref, q_out),), out_sems.at[pl.ds(0, 1)])
    loads[2].wait()
    t_ref[...] = wk[...].T
    project(x_ref, ((t_ref, k_ref),))
    stores += start(((k_ref, k_out),), out_sems.at[pl.ds(1, 1)])
    pair_products(place_ref[0], scale, q_ref, k_ref, own_ref, other_ref)
    for store in stores:
        store.wait()


def value_kernel(x_ref, w_ref, v_ref, t_ref):
    t_ref[...] = w_ref[...].T
    project(x_ref, ((t_ref, v_ref),))


def grad_rows_kernel(place_ref, c_ref, w_in, v_in, g_out, own_ref, other_ref, w, v_ref, g_ref, in_sems, out_sems):
    loads = start(((w_in, w), (v_in, v_ref)), in_sems)
    loads[0].wait()
    project(c_ref, ((w, g_ref),))
    stores = start(((g_ref, g_out),), out_sems)
    loads[1].wait()
    pair_products(place_ref[0], None, g_ref, v_ref, own_ref, other_ref)
    stores[0].wait()


def split_kernel(place_ref, a_ref, b_ref, *outs):
    rows = outs[0].shape[0]
    for d, ref in enumerate(outs):
        at = pl.ds(pl.multiple_of(lax.rem(place_ref[1] + d, len(outs)) * rows, rows), rows)
        ref[...] = (a_ref[at] + b_ref[at]).astype(ref.dtype)


def sum_kernel(*refs):
    a, b, c, d, out_ref = refs
    out_ref[...] = (a[...] + b[...]) + (c[...] + d[...])


def fold_kernel(place_ref, logit_ref, *refs):
    grads, outs = refs[:4], refs[4:]
    rows = outs[0].shape[0] // 2
    for d, ref in enumerate(outs):
        at = pl.ds(pl.multiple_of(lax.rem(place_ref[2] + d, len(outs)) * rows, rows), rows)
        a, b, c, e = (grad[at].astype(F32) for grad in grads)
        ref[pl.ds(0, rows)] = logit_ref[at]
        ref[pl.ds(rows, rows)] = (a + b) + (c + e)


def softmax_kernel(scaling, a_ref, b_ref, c_ref, d_ref, out_ref):
    total = (a_ref[...] + b_ref[...]) + (c_ref[...] + d_ref[...])
    rows = total.shape[0] // 2
    logit, grad = total[:rows], total[rows:]
    exponent = jnp.exp(logit - jnp.max(logit, axis=-1, keepdims=True))
    prob = (exponent / jnp.sum(exponent, axis=-1, keepdims=True)).astype(BF16)
    weights = prob.astype(F32)
    row_dot = jnp.sum(weights * grad, axis=-1, keepdims=True)
    out_ref[pl.ds(0, rows)] = prob
    out_ref[pl.ds(rows, rows)] = (scaling * weights * (grad - row_dot)).astype(BF16)


def fetch_kernel(*refs):
    count = (len(refs) - 1) // 2
    for copy in start(list(zip(refs[:count], refs[count:-1])), refs[-1]):
        copy.wait()


def join_kernel(place_ref, *refs):
    parts, out_ref = refs[:4], refs[-1]
    rows = out_ref.shape[1] // len(parts)
    for d, part_ref in enumerate(parts):
        first = lax.rem(place_ref[2] + len(parts) - d, len(parts)) * rows
        at = pl.ds(pl.multiple_of(first, rows), rows)
        for term in range(2):
            out_ref[term, at] = part_ref[pl.ds(term * rows, rows)]


def place_rows(here, parts, stage_ref):
    rows = parts[0].shape[1]
    for d, part_ref in enumerate(parts):
        first = lax.rem(here + len(parts) - d, len(parts)) * rows
        stage_ref[:, pl.ds(pl.multiple_of(first, rows), rows)] = part_ref[...]


def head_grads(base, q_ref, k_ref, g_ref, outs, stage_ref):
    res = stage_ref.shape[-1]
    for h in range(q_ref.shape[0] // 2):
        prob, logit_grad = (stage_ref[term, pl.ds(h * res, res)] for term in range(2))
        hh = base + h
        for o_ref, value in zip(
            outs,
            (dot(k_ref[hh], logit_grad, NT), dot(q_ref[hh], logit_grad), dot(g_ref[hh], prob)),
        ):
            o_ref[:, hh] = value.astype(BF16).reshape(o_ref.shape[0], -1, res)


def output_kernel(place_ref, *refs):
    own, other, held, weights, out_ref = refs[:4], refs[4:8], refs[8:11], refs[11:14], refs[14]
    outs, own_stage, other_stage = refs[15:18], refs[18], refs[19]
    core = place_ref[0]
    half = held[0].shape[0] // 2
    place_rows(place_ref[1], own, own_stage)
    head_grads(core * half, *held, outs, own_stage)
    place_rows(place_ref[3], other, other_stage)
    head_grads((1 - core) * half, *held, outs, other_stage)
    res = held[0].shape[-1]
    for s in range(out_ref.shape[1]):
        total = None
        for w_ref, o_ref in zip(weights, outs):
            part = dot(w_ref[...], o_ref[s].reshape(-1, res))
            total = part if total is None else total + part
        out_ref[:, s] = total.astype(BF16).T.reshape(out_ref.shape[0], -1, out_ref.shape[-1])


def call(kernel, outs, *args, specs=None, out_specs=None, scratch=(), mib=16):
    return pl.pallas_call(
        kernel,
        out_shape=outs,
        in_specs=list(specs or [VMEM] * len(args)),
        out_specs=out_specs or jax.tree.map(lambda _: VMEM, outs),
        scratch_shapes=scratch,
        compiler_params=pltpu.CompilerParams(vmem_limit_bytes=mib * 1024 * 1024),
    )(*args)


def shape(dims, dtype=BF16):
    return jax.ShapeDtypeStruct(dims, dtype)


def shift(a, axis, step):
    n = lax.axis_size(axis)
    return lax.ppermute(a, axis, [(i, (i + step) % n) for i in range(n)])


AXES = ("x", "core", "z", "y")


def number(x, core, z, y):
    return x * 32 + core * 16 + z * 4 + y


def turn(stage, step):
    pairs = []
    for core, axes in ((0, "xzy"), (1, "yxz")):
        for n in range(64):
            at = dict(x=n // 16, z=n // 4 % 4, y=n % 4)
            to = dict(at)
            to[axes[stage]] = (at[axes[stage]] + step) % 4
            pairs.append((number(core=core, **at), number(core=core, **to)))
    return pairs


def body(normed, cotangent, w_query, w_key, w_value, w_out):
    blocks = lax.axis_size(("z", "y"))
    seq_count, block, width = normed.shape
    seqs, res = seq_count // blocks, block * blocks
    head = width // HEADS
    half = HEADS // 2
    scaling = 1.0 / math.sqrt(head * seqs * lax.axis_size(AXES))
    core, x, z, y = (lax.axis_index(axis) for axis in ("core", "x", "z", "y"))
    place = jnp.stack(
        [core, jnp.where(core == 0, x, y), jnp.where(core == 0, z, x), jnp.where(core == 0, y, x)]
    ).astype(jnp.int32)

    def exchange(a):
        return lax.all_to_all(a, ("z", "y"), split_axis=0, concat_axis=0, tiled=True)

    def spread(parts, stage):
        sent = {d: lax.ppermute(parts[d], AXES, turn(stage, d)) for d in (1, 3, 2)}
        return [parts[0]] + [sent[d] for d in (1, 2, 3)]

    def flat(a):
        return a.reshape(half * res, res)

    rows = exchange(normed.reshape(blocks, seqs, block, width))
    cot_rows = exchange(cotangent.reshape(blocks, seqs, block, width))
    packed = shape((HEADS, seqs * head, res))
    sums = shape((half, res, res), F32)
    quarter = (half * res // 4, res)
    weight, held = pltpu.VMEM((width, width), BF16), pltpu.VMEM(packed.shape, BF16)
    sems = pltpu.SemaphoreType.DMA

    def split(dtype, own, other):
        return call(
            split_kernel, [shape(quarter, dtype)] * 4, place, flat(own), flat(shift(other, "core", 1)),
            specs=(SMEM, VMEM, VMEM),
        )

    def row_part(rows, *weights):
        q, k, own, other = call(
            lambda *refs: rows_kernel(scaling, *refs),
            (packed, packed, sums, sums),
            place, rows, *weights[:2],
            specs=(SMEM, HBM, HBM, HBM), out_specs=(HBM, HBM, VMEM, VMEM),
            scratch=[weight] * 3
            + [pltpu.VMEM((blocks, seqs, block, width), BF16)]
            + [held] * 2
            + [sems((3,)), sems((2,))],
            mib=24,
        )
        v = call(value_kernel, packed, rows, weights[2], scratch=[weight])
        return q, k, v, call(sum_kernel, shape(quarter, F32), *spread(split(F32, own, other), 0))

    def no_part(*_):
        return *(jnp.zeros(packed.shape, BF16) for _ in range(3)), jnp.zeros(quarter, F32)

    q, k, v, logit = lax.cond(core < 2, row_part, no_part, rows, w_query, w_key, w_value)
    g, grad_own, grad_other = call(
        grad_rows_kernel, (packed, sums, shape(sums.shape)), place, cot_rows, w_out, v,
        specs=(SMEM, VMEM, HBM, HBM), out_specs=(HBM, VMEM, VMEM),
        scratch=[weight, held, held, sems((2,)), sems((1,))],
    )
    grads = spread(split(BF16, grad_own, grad_other), 0)
    both = (quarter[0] // 2, res)
    terms = call(
        fold_kernel, [shape(both, F32)] * 4, place, logit, *grads, specs=[SMEM] + [VMEM] * 5
    )
    term = call(sum_kernel, shape(both, F32), *spread(terms, 1))
    result = call(
        lambda *refs: softmax_kernel(scaling, *refs), shape(both), *spread([term] * 4, 2)
    )
    q, k, g = call(
        fetch_kernel, [packed] * 3, q, k, g, specs=[HBM] * 3, scratch=[sems((3,))]
    )
    result = call(
        join_kernel, shape((2,) + quarter), place, *spread([result] * 4, 1), q,
        specs=[SMEM] + [VMEM] * 4 + [ANY],
    )
    own = spread([result] * 4, 0)
    other = [shift(a, "core", 1) for a in own]
    grown = pltpu.VMEM((seqs, HEADS, head, res), BF16)
    out = call(
        output_kernel,
        shape((blocks, seqs, block, width)),
        place, *own, *other, q, k, g, w_query, w_key, w_value,
        specs=[SMEM] + [VMEM] * 14,
        scratch=[grown] * 3 + [pltpu.VMEM((2, half * res, res), BF16)] * 2,
        mib=24,
    )
    return exchange(out).reshape(seq_count, block, width)


def solution(mesh):
    fine = Mesh(mesh.devices.reshape(4, 2, 4, 4), ("x", "core", "z", "y"))
    spec = P(("x", "core"), ("z", "y"), None)
    return jax.shard_map(
        body, mesh=fine, in_specs=(spec, spec, P(), P(), P(), P()), out_specs=spec, check_vma=False
    )
```

```python
import math

import jax
import jax.numpy as jnp
from jax import lax
from jax.experimental import pallas as pl
from jax.experimental.pallas import tpu as pltpu
from jax.sharding import Mesh, PartitionSpec as P

HEADS = 12
F32 = jnp.float32
BF16 = jnp.bfloat16
VMEM = pl.BlockSpec(memory_space=pltpu.VMEM)
SMEM = pl.BlockSpec(memory_space=pltpu.SMEM)
ANY = pl.BlockSpec(memory_space=pl.ANY)
HBM = pl.BlockSpec(memory_space=pltpu.HBM)
NT = (((1,), (1,)), ((), ()))
TN = (((0,), (0,)), ((), ()))


def dot(a, b, dims=(((1,), (0,)), ((), ()))):
    return lax.dot_general(a, b, dims, preferred_element_type=F32)


def project(x_ref, pairs):
    blocks, seqs, block, width = x_ref.shape
    for s in range(seqs):
        rows = x_ref[:, s].reshape(blocks * block, width)
        for w_ref, o_ref in pairs:
            heads, packed, res = o_ref.shape
            head = packed // seqs
            out = dot(w_ref[...], rows, NT).astype(BF16)
            o_ref[:, s * head : (s + 1) * head, :] = out.reshape(heads, head, res)


def pair_products(core, scale, a_ref, b_ref, own_ref, other_ref):
    half = own_ref.shape[0]
    for h in range(half):
        for ref, base in ((own_ref, core * half), (other_ref, (1 - core) * half)):
            product = dot(a_ref[base + h], b_ref[base + h], TN)
            ref[h] = (product if scale is None else scale * product).astype(ref.dtype)


def start(pairs, sems):
    copies = [pltpu.make_async_copy(src, dst, sems.at[n]) for n, (src, dst) in enumerate(pairs)]
    for copy in copies:
        copy.start()
    return copies


def rows_kernel(scale, place_ref, x_in, wq_in, wk_in, q_out, k_out, own_ref, other_ref, wq, wk, t_ref, x_ref, q_ref, k_ref, in_sems, out_sems):
    loads = start(((wq_in, wq), (x_in, x_ref), (wk_in, wk)), in_sems)
    loads[0].wait()
    t_ref[...] = wq[...].T
    loads[1].wait()
    project(x_ref, ((t_ref, q_ref),))
    stores = start(((q_ref, q_out),), out_sems.at[pl.ds(0, 1)])
    loads[2].wait()
    t_ref[...] = wk[...].T
    project(x_ref, ((t_ref, k_ref),))
    stores += start(((k_ref, k_out),), out_sems.at[pl.ds(1, 1)])
    pair_products(place_ref[0], scale, q_ref, k_ref, own_ref, other_ref)
    for store in stores:
        store.wait()


def value_kernel(x_ref, w_ref, v_ref, t_ref):
    t_ref[...] = w_ref[...].T
    project(x_ref, ((t_ref, v_ref),))


def grad_rows_kernel(place_ref, c_ref, w_in, v_in, g_out, own_ref, other_ref, w, v_ref, g_ref, in_sems, out_sems):
    loads = start(((w_in, w), (v_in, v_ref)), in_sems)
    loads[0].wait()
    project(c_ref, ((w, g_ref),))
    stores = start(((g_ref, g_out),), out_sems)
    loads[1].wait()
    pair_products(place_ref[0], None, g_ref, v_ref, own_ref, other_ref)
    stores[0].wait()


def split_kernel(place_ref, a_ref, b_ref, *outs):
    rows = outs[0].shape[0]
    for d, ref in enumerate(outs):
        at = pl.ds(pl.multiple_of(lax.rem(place_ref[1] + d, len(outs)) * rows, rows), rows)
        ref[...] = (a_ref[at] + b_ref[at]).astype(ref.dtype)


def sum_kernel(*refs):
    a, b, c, d, out_ref = refs
    out_ref[...] = (a[...] + b[...]) + (c[...] + d[...])


def fold_kernel(place_ref, logit_ref, *refs):
    grads, outs = refs[:4], refs[4:]
    rows = outs[0].shape[0] // 2
    for d, ref in enumerate(outs):
        at = pl.ds(pl.multiple_of(lax.rem(place_ref[2] + d, len(outs)) * rows, rows), rows)
        a, b, c, e = (grad[at].astype(F32) for grad in grads)
        ref[pl.ds(0, rows)] = logit_ref[at]
        ref[pl.ds(rows, rows)] = (a + b) + (c + e)


def softmax_kernel(scaling, a_ref, b_ref, c_ref, d_ref, out_ref):
    total = (a_ref[...] + b_ref[...]) + (c_ref[...] + d_ref[...])
    rows = total.shape[0] // 2
    logit, grad = total[:rows], total[rows:]
    exponent = jnp.exp(logit - jnp.max(logit, axis=-1, keepdims=True))
    prob = (exponent / jnp.sum(exponent, axis=-1, keepdims=True)).astype(BF16)
    weights = prob.astype(F32)
    row_dot = jnp.sum(weights * grad, axis=-1, keepdims=True)
    out_ref[pl.ds(0, rows)] = prob
    out_ref[pl.ds(rows, rows)] = (scaling * weights * (grad - row_dot)).astype(BF16)


def fetch_kernel(*refs):
    count = (len(refs) - 1) // 2
    for copy in start(list(zip(refs[:count], refs[count:-1])), refs[-1]):
        copy.wait()


def join_kernel(place_ref, *refs):
    parts, out_ref = refs[:4], refs[-1]
    rows = out_ref.shape[1] // len(parts)
    for d, part_ref in enumerate(parts):
        first = lax.rem(place_ref[2] + len(parts) - d, len(parts)) * rows
        at = pl.ds(pl.multiple_of(first, rows), rows)
        for term in range(2):
            out_ref[term, at] = part_ref[pl.ds(term * rows, rows)]


def place_rows(here, parts, stage_ref):
    rows = parts[0].shape[1]
    for d, part_ref in enumerate(parts):
        first = lax.rem(here + len(parts) - d, len(parts)) * rows
        stage_ref[:, pl.ds(pl.multiple_of(first, rows), rows)] = part_ref[...]


def head_grads(base, first, q_ref, k_ref, g_ref, outs, stage_ref):
    res = stage_ref.shape[-1]
    for h in range(q_ref.shape[0] // 2):
        prob, logit_grad = (stage_ref[term, pl.ds(h * res, res)] for term in range(2))
        hh = base + h
        for o_ref, value in zip(
            outs,
            (dot(k_ref[hh], logit_grad, NT), dot(q_ref[hh], logit_grad), dot(g_ref[hh], prob)),
        ):
            o_ref[:, first + h] = value.astype(BF16).reshape(o_ref.shape[0], -1, res)


def own_grads_kernel(place_ref, *refs):
    own, held, outs, stage_ref = refs[:4], refs[4:7], refs[7:10], refs[10]
    place_rows(place_ref[1], own, stage_ref)
    head_grads(place_ref[0] * outs[0].shape[1], 0, *held, outs, stage_ref)


def output_kernel(place_ref, *refs):
    other, own_outs, held, weights, out_ref = refs[:4], refs[4:7], refs[7:10], refs[10:13], refs[13]
    outs, stage_ref = refs[14:17], refs[17]
    core = place_ref[0]
    half = held[0].shape[0] // 2
    for own_ref, o_ref in zip(own_outs, outs):
        o_ref[:, pl.ds(core * half, half)] = own_ref[...]
    place_rows(place_ref[3], other, stage_ref)
    head_grads((1 - core) * half, (1 - core) * half, *held, outs, stage_ref)
    res = held[0].shape[-1]
    for s in range(out_ref.shape[1]):
        total = None
        for w_ref, o_ref in zip(weights, outs):
            part = dot(w_ref[...], o_ref[s].reshape(-1, res))
            total = part if total is None else total + part
        out_ref[:, s] = total.astype(BF16).T.reshape(out_ref.shape[0], -1, out_ref.shape[-1])


def call(kernel, outs, *args, specs=None, out_specs=None, scratch=(), mib=16):
    return pl.pallas_call(
        kernel,
        out_shape=outs,
        in_specs=list(specs or [VMEM] * len(args)),
        out_specs=out_specs or jax.tree.map(lambda _: VMEM, outs),
        scratch_shapes=scratch,
        compiler_params=pltpu.CompilerParams(vmem_limit_bytes=mib * 1024 * 1024),
    )(*args)


def shape(dims, dtype=BF16):
    return jax.ShapeDtypeStruct(dims, dtype)


def shift(a, axis, step):
    n = lax.axis_size(axis)
    return lax.ppermute(a, axis, [(i, (i + step) % n) for i in range(n)])


AXES = ("x", "core", "z", "y")


def number(x, core, z, y):
    return x * 32 + core * 16 + z * 4 + y


def turn(stage, step):
    pairs = []
    for core, axes in ((0, "xzy"), (1, "yxz")):
        for n in range(64):
            at = dict(x=n // 16, z=n // 4 % 4, y=n % 4)
            to = dict(at)
            to[axes[stage]] = (at[axes[stage]] + step) % 4
            pairs.append((number(core=core, **at), number(core=core, **to)))
    return pairs


def body(normed, cotangent, w_query, w_key, w_value, w_out):
    blocks = lax.axis_size(("z", "y"))
    seq_count, block, width = normed.shape
    seqs, res = seq_count // blocks, block * blocks
    head = width // HEADS
    half = HEADS // 2
    scaling = 1.0 / math.sqrt(head * seqs * lax.axis_size(AXES))
    core, x, z, y = (lax.axis_index(axis) for axis in ("core", "x", "z", "y"))
    place = jnp.stack(
        [core, jnp.where(core == 0, x, y), jnp.where(core == 0, z, x), jnp.where(core == 0, y, x)]
    ).astype(jnp.int32)

    def exchange(a):
        return lax.all_to_all(a, ("z", "y"), split_axis=0, concat_axis=0, tiled=True)

    def spread(parts, stage):
        sent = {d: lax.ppermute(parts[d], AXES, turn(stage, d)) for d in (1, 3, 2)}
        return [parts[0]] + [sent[d] for d in (1, 2, 3)]

    def flat(a):
        return a.reshape(half * res, res)

    rows = exchange(normed.reshape(blocks, seqs, block, width))
    cot_rows = exchange(cotangent.reshape(blocks, seqs, block, width))
    packed = shape((HEADS, seqs * head, res))
    sums = shape((half, res, res), F32)
    quarter = (half * res // 4, res)
    weight, held = pltpu.VMEM((width, width), BF16), pltpu.VMEM(packed.shape, BF16)
    sems = pltpu.SemaphoreType.DMA

    def split(dtype, own, other):
        return call(
            split_kernel, [shape(quarter, dtype)] * 4, place, flat(own), flat(shift(other, "core", 1)),
            specs=(SMEM, VMEM, VMEM),
        )

    def row_part(rows, *weights):
        q, k, own, other = call(
            lambda *refs: rows_kernel(scaling, *refs),
            (packed, packed, sums, sums),
            place, rows, *weights[:2],
            specs=(SMEM, HBM, HBM, HBM), out_specs=(HBM, HBM, VMEM, VMEM),
            scratch=[weight] * 3
            + [pltpu.VMEM((blocks, seqs, block, width), BF16)]
            + [held] * 2
            + [sems((3,)), sems((2,))],
            mib=24,
        )
        v = call(value_kernel, packed, rows, weights[2], scratch=[weight])
        return q, k, v, call(sum_kernel, shape(quarter, F32), *spread(split(F32, own, other), 0))

    def no_part(*_):
        return *(jnp.zeros(packed.shape, BF16) for _ in range(3)), jnp.zeros(quarter, F32)

    q, k, v, logit = lax.cond(core < 2, row_part, no_part, rows, w_query, w_key, w_value)
    g, grad_own, grad_other = call(
        grad_rows_kernel, (packed, sums, shape(sums.shape)), place, cot_rows, w_out, v,
        specs=(SMEM, VMEM, HBM, HBM), out_specs=(HBM, VMEM, VMEM),
        scratch=[weight, held, held, sems((2,)), sems((1,))],
    )
    grads = spread(split(BF16, grad_own, grad_other), 0)
    both = (quarter[0] // 2, res)
    terms = call(
        fold_kernel, [shape(both, F32)] * 4, place, logit, *grads, specs=[SMEM] + [VMEM] * 5
    )
    term = call(sum_kernel, shape(both, F32), *spread(terms, 1))
    result = call(
        lambda *refs: softmax_kernel(scaling, *refs), shape(both), *spread([term] * 4, 2)
    )
    q, k, g = call(
        fetch_kernel, [packed] * 3, q, k, g, specs=[HBM] * 3, scratch=[sems((3,))]
    )
    result = call(
        join_kernel, shape((2,) + quarter), place, *spread([result] * 4, 1), q,
        specs=[SMEM] + [VMEM] * 4 + [ANY],
    )
    own = spread([result] * 4, 0)
    other = [shift(a, "core", 1) for a in own]
    stage = pltpu.VMEM((2, half * res, res), BF16)
    own_grown = call(
        own_grads_kernel, [shape((seqs, half, head, res))] * 3, place, *own, q, k, g,
        specs=[SMEM] + [VMEM] * 7, scratch=[stage],
    )
    out = call(
        output_kernel,
        shape((blocks, seqs, block, width)),
        place, *other, *own_grown, q, k, g, w_query, w_key, w_value,
        specs=[SMEM] + [VMEM] * 13,
        scratch=[pltpu.VMEM((seqs, HEADS, head, res), BF16)] * 3 + [stage],
        mib=24,
    )
    return exchange(out).reshape(seq_count, block, width)


def solution(mesh):
    fine = Mesh(mesh.devices.reshape(4, 2, 4, 4), ("x", "core", "z", "y"))
    spec = P(("x", "core"), ("z", "y"), None)
    return jax.shard_map(
        body, mesh=fine, in_specs=(spec, spec, P(), P(), P(), P()), out_specs=spec, check_vma=False
    )
```

```python
import math

import jax
import jax.numpy as jnp
from jax import lax
from jax.experimental import pallas as pl
from jax.experimental.pallas import tpu as pltpu
from jax.sharding import Mesh, PartitionSpec as P

HEADS = 12
F32 = jnp.float32
BF16 = jnp.bfloat16
VMEM = pl.BlockSpec(memory_space=pltpu.VMEM)
SMEM = pl.BlockSpec(memory_space=pltpu.SMEM)
ANY = pl.BlockSpec(memory_space=pl.ANY)
HBM = pl.BlockSpec(memory_space=pltpu.HBM)
NT = (((1,), (1,)), ((), ()))
TN = (((0,), (0,)), ((), ()))


def dot(a, b, dims=(((1,), (0,)), ((), ()))):
    return lax.dot_general(a, b, dims, preferred_element_type=F32)


def project(x_ref, pairs):
    blocks, seqs, block, width = x_ref.shape
    for s in range(seqs):
        rows = x_ref[:, s].reshape(blocks * block, width)
        for w_ref, o_ref in pairs:
            heads, packed, res = o_ref.shape
            head = packed // seqs
            out = dot(w_ref[...], rows, NT).astype(BF16)
            o_ref[:, s * head : (s + 1) * head, :] = out.reshape(heads, head, res)


def half_products(base, scale, a_ref, b_ref, out_ref):
    for h in range(out_ref.shape[0]):
        product = dot(a_ref[base + h], b_ref[base + h], TN)
        out_ref[h] = (product if scale is None else scale * product).astype(out_ref.dtype)


def start(pairs, sems):
    copies = [pltpu.make_async_copy(src, dst, sems.at[n]) for n, (src, dst) in enumerate(pairs)]
    for copy in copies:
        copy.start()
    return copies


def rows_kernel(scale, place_ref, x_in, wq_in, wk_in, q_ref, k_ref, other_ref, wq, wk, t_ref, x_ref, sems):
    loads = start(((wq_in, wq), (x_in, x_ref), (wk_in, wk)), sems)
    loads[0].wait()
    t_ref[...] = wq[...].T
    loads[1].wait()
    project(x_ref, ((t_ref, q_ref),))
    loads[2].wait()
    t_ref[...] = wk[...].T
    project(x_ref, ((t_ref, k_ref),))
    half_products((1 - place_ref[0]) * other_ref.shape[0], scale, q_ref, k_ref, other_ref)


def own_rows_kernel(scale, place_ref, q_ref, k_ref, q_out, k_out, own_ref, sems):
    stores = start(((q_ref, q_out), (k_ref, k_out)), sems)
    half_products(place_ref[0] * own_ref.shape[0], scale, q_ref, k_ref, own_ref)
    for store in stores:
        store.wait()


def value_kernel(x_ref, w_ref, v_ref, t_ref):
    t_ref[...] = w_ref[...].T
    project(x_ref, ((t_ref, v_ref),))


def grad_rows_kernel(place_ref, c_ref, w_in, v_in, g_ref, v_ref, other_ref, w, sems):
    loads = start(((w_in, w), (v_in, v_ref)), sems)
    loads[0].wait()
    project(c_ref, ((w, g_ref),))
    loads[1].wait()
    half_products((1 - place_ref[0]) * other_ref.shape[0], None, g_ref, v_ref, other_ref)


def own_grad_kernel(place_ref, g_ref, v_ref, own_ref):
    half_products(place_ref[0] * own_ref.shape[0], None, g_ref, v_ref, own_ref)


def split_kernel(place_ref, a_ref, b_ref, *outs):
    rows = outs[0].shape[0]
    for d, ref in enumerate(outs):
        at = pl.ds(pl.multiple_of(lax.rem(place_ref[1] + d, len(outs)) * rows, rows), rows)
        ref[...] = (a_ref[at] + b_ref[at]).astype(ref.dtype)


def sum_kernel(*refs):
    a, b, c, d, out_ref = refs
    out_ref[...] = (a[...] + b[...]) + (c[...] + d[...])


def fold_kernel(place_ref, logit_ref, *refs):
    grads, outs = refs[:4], refs[4:]
    rows = outs[0].shape[0] // 2
    for d, ref in enumerate(outs):
        at = pl.ds(pl.multiple_of(lax.rem(place_ref[2] + d, len(outs)) * rows, rows), rows)
        a, b, c, e = (grad[at].astype(F32) for grad in grads)
        ref[pl.ds(0, rows)] = logit_ref[at]
        ref[pl.ds(rows, rows)] = (a + b) + (c + e)


def softmax_kernel(scaling, a_ref, b_ref, c_ref, d_ref, out_ref):
    total = (a_ref[...] + b_ref[...]) + (c_ref[...] + d_ref[...])
    rows = total.shape[0] // 2
    logit, grad = total[:rows], total[rows:]
    exponent = jnp.exp(logit - jnp.max(logit, axis=-1, keepdims=True))
    prob = (exponent / jnp.sum(exponent, axis=-1, keepdims=True)).astype(BF16)
    weights = prob.astype(F32)
    row_dot = jnp.sum(weights * grad, axis=-1, keepdims=True)
    out_ref[pl.ds(0, rows)] = prob
    out_ref[pl.ds(rows, rows)] = (scaling * weights * (grad - row_dot)).astype(BF16)


def fetch_kernel(*refs):
    count = (len(refs) - 1) // 2
    for copy in start(list(zip(refs[:count], refs[count:-1])), refs[-1]):
        copy.wait()


def join_kernel(place_ref, *refs):
    parts, out_ref = refs[:4], refs[-1]
    rows = out_ref.shape[1] // len(parts)
    for d, part_ref in enumerate(parts):
        first = lax.rem(place_ref[2] + len(parts) - d, len(parts)) * rows
        at = pl.ds(pl.multiple_of(first, rows), rows)
        for term in range(2):
            out_ref[term, at] = part_ref[pl.ds(term * rows, rows)]


def place_rows(here, parts, stage_ref):
    rows = parts[0].shape[1]
    for d, part_ref in enumerate(parts):
        first = lax.rem(here + len(parts) - d, len(parts)) * rows
        stage_ref[:, pl.ds(pl.multiple_of(first, rows), rows)] = part_ref[...]


def head_grads(base, q_ref, k_ref, g_ref, outs, stage_ref):
    res = stage_ref.shape[-1]
    for h in range(q_ref.shape[0] // 2):
        prob, logit_grad = (stage_ref[term, pl.ds(h * res, res)] for term in range(2))
        hh = base + h
        for o_ref, value in zip(
            outs,
            (dot(k_ref[hh], logit_grad, NT), dot(q_ref[hh], logit_grad), dot(g_ref[hh], prob)),
        ):
            o_ref[:, hh] = value.astype(BF16).reshape(o_ref.shape[0], -1, res)


def output_kernel(place_ref, *refs):
    own, other, held, weights, out_ref = refs[:4], refs[4:8], refs[8:11], refs[11:14], refs[14]
    outs, own_stage, other_stage = refs[15:18], refs[18], refs[19]
    core = place_ref[0]
    half = held[0].shape[0] // 2
    place_rows(place_ref[1], own, own_stage)
    head_grads(core * half, *held, outs, own_stage)
    place_rows(place_ref[3], other, other_stage)
    head_grads((1 - core) * half, *held, outs, other_stage)
    res = held[0].shape[-1]
    for s in range(out_ref.shape[1]):
        total = None
        for w_ref, o_ref in zip(weights, outs):
            part = dot(w_ref[...], o_ref[s].reshape(-1, res))
            total = part if total is None else total + part
        out_ref[:, s] = total.astype(BF16).T.reshape(out_ref.shape[0], -1, out_ref.shape[-1])


def call(kernel, outs, *args, specs=None, out_specs=None, scratch=(), mib=16):
    return pl.pallas_call(
        kernel,
        out_shape=outs,
        in_specs=list(specs or [VMEM] * len(args)),
        out_specs=out_specs or jax.tree.map(lambda _: VMEM, outs),
        scratch_shapes=scratch,
        compiler_params=pltpu.CompilerParams(vmem_limit_bytes=mib * 1024 * 1024),
    )(*args)


def shape(dims, dtype=BF16):
    return jax.ShapeDtypeStruct(dims, dtype)


def shift(a, axis, step):
    n = lax.axis_size(axis)
    return lax.ppermute(a, axis, [(i, (i + step) % n) for i in range(n)])


AXES = ("x", "core", "z", "y")


def number(x, core, z, y):
    return x * 32 + core * 16 + z * 4 + y


def turn(stage, step):
    pairs = []
    for core, axes in ((0, "xzy"), (1, "yxz")):
        for n in range(64):
            at = dict(x=n // 16, z=n // 4 % 4, y=n % 4)
            to = dict(at)
            to[axes[stage]] = (at[axes[stage]] + step) % 4
            pairs.append((number(core=core, **at), number(core=core, **to)))
    return pairs


def body(normed, cotangent, w_query, w_key, w_value, w_out):
    blocks = lax.axis_size(("z", "y"))
    seq_count, block, width = normed.shape
    seqs, res = seq_count // blocks, block * blocks
    head = width // HEADS
    half = HEADS // 2
    scaling = 1.0 / math.sqrt(head * seqs * lax.axis_size(AXES))
    core, x, z, y = (lax.axis_index(axis) for axis in ("core", "x", "z", "y"))
    place = jnp.stack(
        [core, jnp.where(core == 0, x, y), jnp.where(core == 0, z, x), jnp.where(core == 0, y, x)]
    ).astype(jnp.int32)

    def exchange(a):
        return lax.all_to_all(a, ("z", "y"), split_axis=0, concat_axis=0, tiled=True)

    def spread(parts, stage):
        sent = {d: lax.ppermute(parts[d], AXES, turn(stage, d)) for d in (1, 3, 2)}
        return [parts[0]] + [sent[d] for d in (1, 2, 3)]

    def flat(a):
        return a.reshape(half * res, res)

    rows = exchange(normed.reshape(blocks, seqs, block, width))
    cot_rows = exchange(cotangent.reshape(blocks, seqs, block, width))
    packed = shape((HEADS, seqs * head, res))
    sums = shape((half, res, res), F32)
    quarter = (half * res // 4, res)
    weight, held = pltpu.VMEM((width, width), BF16), pltpu.VMEM(packed.shape, BF16)
    sems = pltpu.SemaphoreType.DMA

    def split(dtype, own, other):
        return call(
            split_kernel, [shape(quarter, dtype)] * 4, place, flat(own), flat(shift(other, "core", 1)),
            specs=(SMEM, VMEM, VMEM),
        )

    def row_part(rows, *weights):
        q, k, other = call(
            lambda *refs: rows_kernel(scaling, *refs),
            (packed, packed, sums),
            place, rows, *weights[:2],
            specs=(SMEM, HBM, HBM, HBM),
            scratch=[weight] * 3 + [pltpu.VMEM((blocks, seqs, block, width), BF16), sems((3,))],
            mib=24,
        )
        q, k, own = call(
            lambda *refs: own_rows_kernel(scaling, *refs),
            (packed, packed, sums),
            place, q, k,
            specs=(SMEM, VMEM, VMEM), out_specs=(HBM, HBM, VMEM), scratch=[sems((2,))],
        )
        v = call(value_kernel, packed, rows, weights[2], scratch=[weight])
        return q, k, v, call(sum_kernel, shape(quarter, F32), *spread(split(F32, own, other), 0))

    def no_part(*_):
        return *(jnp.zeros(packed.shape, BF16) for _ in range(3)), jnp.zeros(quarter, F32)

    q, k, v, logit = lax.cond(core < 2, row_part, no_part, rows, w_query, w_key, w_value)
    g, v, grad_other = call(
        grad_rows_kernel, (packed, packed, shape(sums.shape)), place, cot_rows, w_out, v,
        specs=(SMEM, VMEM, HBM, HBM), scratch=[weight, sems((2,))],
    )
    grad_own = call(own_grad_kernel, sums, place, g, v, specs=(SMEM, VMEM, VMEM))
    grads = spread(split(BF16, grad_own, grad_other), 0)
    both = (quarter[0] // 2, res)
    terms = call(
        fold_kernel, [shape(both, F32)] * 4, place, logit, *grads, specs=[SMEM] + [VMEM] * 5
    )
    term = call(sum_kernel, shape(both, F32), *spread(terms, 1))
    result = call(
        lambda *refs: softmax_kernel(scaling, *refs), shape(both), *spread([term] * 4, 2)
    )
    q, k = call(fetch_kernel, [packed] * 2, q, k, specs=[HBM] * 2, scratch=[sems((2,))])
    result = call(
        join_kernel, shape((2,) + quarter), place, *spread([result] * 4, 1), q,
        specs=[SMEM] + [VMEM] * 4 + [ANY],
    )
    own = spread([result] * 4, 0)
    other = [shift(a, "core", 1) for a in own]
    grown = pltpu.VMEM((seqs, HEADS, head, res), BF16)
    out = call(
        output_kernel,
        shape((blocks, seqs, block, width)),
        place, *own, *other, q, k, g, w_query, w_key, w_value,
        specs=[SMEM] + [VMEM] * 14,
        scratch=[grown] * 3 + [pltpu.VMEM((2, half * res, res), BF16)] * 2,
        mib=24,
    )
    return exchange(out).reshape(seq_count, block, width)


def solution(mesh):
    fine = Mesh(mesh.devices.reshape(4, 2, 4, 4), ("x", "core", "z", "y"))
    spec = P(("x", "core"), ("z", "y"), None)
    return jax.shard_map(
        body, mesh=fine, in_specs=(spec, spec, P(), P(), P(), P()), out_specs=spec, check_vma=False
    )
```
